32 devices in a mesh: leaf: 4 (over y, x), row: 2 (over core), col: 4 (over z).
Axes of the slice: x: 2, y: 2, z: 4, core: 2. Of those that a mesh axis runs over, the one named last changes fastest.
Arguments:
- sec_rhs: float32 [4, 7, 64, 2048], P('leaf', None, None, 'row'), may hold values from -6 to 6
- sec_inv: float32 [4, 7, 2048, 2048], P('leaf', None, 'row', 'col'), as said below
- sec_low: float32 [4, 10, 2048, 2048], P('leaf', None, 'row', 'col'), may hold values from -0.09375 to 0.09375
- sec_top: float32 [4, 7, 2048, 2048], P('leaf', None, 'row', 'col'), may hold values from -0.046875 to 0.046875
- sec_rows: int32 [4, 7, 16], P('leaf'), may hold values from 0 to 47, as said below
- top_rhs: float32 [7, 64, 2048], P(None, None, 'row'), may hold values from -6 to 6
- top_inv: float32 [7, 2048, 2048], P(None, 'row', 'col'), as said below
- top_low: float32 [10, 2048, 2048], P(None, 'row', 'col'), may hold values from -0.09375 to 0.09375
- sec_parent: int32 [4], replicated, may hold values from 0 to 3, as said below
- top_parent: int32 [4], replicated, may hold values from 0 to 1, as said below
Outputs:
- sec_sol: float32 [4, 7, 64, 2048], P('leaf', None, None, 'row')
- top_sol: float32 [7, 64, 2048], P(None, None, 'row')
The draws below stay inside these ranges and needn't reach their ends.
Inputs may be any that keep to these rules, and one draw needn't show every extreme that they name: `sec_rows`: within each list the 16 values are distinct. `sec_parent`: each of 0, 1, 2, 3 appears exactly once. `top_parent`: each of 0 and 1 appears exactly twice. `sec_inv`: dense matrices with a positive diagonal; nothing more is promised of their entries. `top_inv`: dense matrices with a positive diagonal; nothing more is promised of their entries.
All inputs are finite; a program needn't handle non-finite values.
Results may differ from the reference program's by a relative error of at most 0.00012.
Values sent between devices are 32-bit elements; how exact they have to be, the bound alone decides.
A program may use at most 192 MiB of HBM per device.

```python
import math
import jax
import jax.numpy as jnp
from jax import lax

BLOCK = 128
NRHS = 64
NBLK = 16
KEEP = 16
W = 2048
SECTIONS = 4


def dense_inverse(key, leading, width):
    key_off, key_diag = jax.random.split(key)
    full_shape = leading + (width, width)
    spread = 0.5 * jax.random.normal(key_off, full_shape, jnp.float32) / math.sqrt(width)
    diagonal_part = jnp.exp(jax.random.uniform(key_diag, leading + (width,), jnp.float32, -0.69, 0.69))
    row_index = lax.broadcasted_iota(jnp.int32, (width, width), 0)
    col_index = lax.broadcasted_iota(jnp.int32, (width, width), 1)
    return jnp.where(row_index == col_index, diagonal_part[..., :, None], spread)


def draw_sec_inv(key, part):
    return dense_inverse(jax.random.fold_in(key, 101), (SECTIONS, 7), W)


def draw_top_inv(key, part):
    return dense_inverse(jax.random.fold_in(key, 202), (7,), W)


def draw_sec_rows(key, part):
    several = jax.random.split(jax.random.fold_in(key, 303), SECTIONS * 7)
    picks = jax.vmap(lambda single: jax.random.permutation(single, 3 * NBLK))(several)
    return picks[:, :KEEP].reshape(SECTIONS, 7, KEEP).astype(jnp.int32)


def draw_sec_parent(key, part):
    return (jax.random.permutation(jax.random.fold_in(key, 404), SECTIONS) % 4).astype(jnp.int32)


def draw_top_parent(key, part):
    return (jax.random.permutation(jax.random.fold_in(key, 505), 4) % 2).astype(jnp.int32)


def block_levels(own_key, extent, shards, smallest, top_value):
    loudness, own = 1.0, jax.random.fold_in(own_key, 6)
    for axis_at, shards_of in shards:
        draws = jnp.exp(jax.random.uniform(jax.random.fold_in(own, axis_at), (shards_of,), jnp.float32, smallest / len(shards), top_value / len(shards)))
        loudness = loudness * jnp.repeat(draws, extent[axis_at] // shards_of).reshape([-1 if axis == axis_at else 1 for axis in range(len(extent))])
    return loudness


def noise(rng, shape, scale, most, pieces=(), held_as=jnp.bfloat16):
    gain = block_levels(rng, shape, pieces, -0.22, 0.18) if pieces else 1.0
    result = jax.random.normal(rng, shape, jnp.float32) * scale * gain
    return jnp.minimum(jnp.maximum(result, -most), most).astype(held_as)


def setup_inputs(seed: int = 0) -> dict:
    streams_of = jax.random.split(jax.random.key(seed), 11)
    sec_rhs = noise(streams_of[0], (SECTIONS, 7, NRHS, W), 1.0, 6.0, ((0, 4), (3, 2)), jnp.float32)
    sec_inv = draw_sec_inv(jax.random.fold_in(streams_of[10], 71), 0)
    sec_low = noise(streams_of[2], (SECTIONS, 10, W, W), (2 * W) ** -0.5, 0.09375, ((0, 4), (2, 2), (3, 4)), jnp.float32)
    sec_top = noise(streams_of[3], (SECTIONS, 7, KEEP * BLOCK, W), (8 * W) ** -0.5, 0.046875, ((0, 4), (2, 2), (3, 4)), jnp.float32)
    sec_rows = draw_sec_rows(jax.random.fold_in(streams_of[10], 71), 0)
    top_rhs = noise(streams_of[5], (7, NRHS, W), 1.0, 6.0, ((2, 2),), jnp.float32)
    top_inv = draw_top_inv(jax.random.fold_in(streams_of[10], 71), 0)
    top_low = noise(streams_of[7], (10, W, W), (2 * W) ** -0.5, 0.09375, ((1, 2), (2, 4)), jnp.float32)
    sec_parent = draw_sec_parent(jax.random.fold_in(streams_of[10], 71), 0)
    top_parent = draw_top_parent(jax.random.fold_in(streams_of[10], 71), 0)
    return {"sec_rhs": sec_rhs, "sec_inv": sec_inv, "sec_low": sec_low, "sec_top": sec_top, "sec_rows": sec_rows, "top_rhs": top_rhs, "top_inv": top_inv, "top_low": top_low, "sec_parent": sec_parent, "top_parent": top_parent}


def apply_block(vectors, matrices):
    return jnp.einsum("btc,brc->btr", vectors, matrices, precision=lax.Precision.HIGHEST)


def reference(sec_rhs, sec_inv, sec_low, sec_top, sec_rows, top_rhs, top_inv, top_low, sec_parent, top_parent):
    node_ids = jnp.arange(7).astype(jnp.int32)
    block_ids = jnp.arange(NBLK).astype(jnp.int32)
    top_update = jnp.zeros((7, NRHS, W), jnp.float32)
    solved = []
    for section in range(SECTIONS):
        right_side = sec_rhs[section]
        inverse = sec_inv[section]
        lower = sec_low[section]
        sol_leaf = apply_block(right_side[0:4], inverse[0:4])
        upward = apply_block(sol_leaf, lower[0:4])
        acc_mid = upward.reshape(2, 2, NRHS, W).sum(1)
        acc_root = apply_block(sol_leaf, lower[4:8]).sum(0, keepdims=True)
        sol_mid = apply_block(right_side[4:6] - acc_mid, inverse[4:6])
        acc_root = acc_root + apply_block(sol_mid, lower[8:10]).sum(0, keepdims=True)
        sol_root = apply_block(right_side[6:7] - acc_root, inverse[6:7])
        whole = jnp.concatenate([sol_leaf, sol_mid, sol_root], axis=0)
        solved.append(whole)
        contrib = apply_block(whole, sec_top[section]).reshape(7, NRHS, KEEP, BLOCK)
        parent_node = sec_parent[section].astype(jnp.int32)
        grand_node = top_parent[parent_node].astype(jnp.int32)
        path_nodes = jnp.stack([parent_node, grand_node + 4, jnp.int32(6)]).astype(jnp.int32)
        row_list = sec_rows[section].astype(jnp.int32)
        node_of = path_nodes[row_list // NBLK]
        sub_block = row_list % NBLK
        one_hot = ((node_of[:, :, None, None] == node_ids[None, None, :, None])
                   & (sub_block[:, :, None, None] == block_ids[None, None, None, :])).astype(jnp.float32)
        placed = jnp.einsum("jtkl,jknm->ntml", contrib, one_hot, precision=lax.Precision.HIGHEST)
        top_update = top_update + placed.reshape(7, NRHS, W)
    sol_three = apply_block(top_rhs[0:4] - top_update[0:4], top_inv[0:4])
    parent_hot = (top_parent[:, None] == jnp.arange(2)[None, :]).astype(jnp.float32)
    to_mid = apply_block(sol_three, top_low[0:8:2])
    acc_four = jnp.einsum("pq,ptr->qtr", parent_hot, to_mid, precision=lax.Precision.HIGHEST)
    acc_top = apply_block(sol_three, top_low[1:8:2]).sum(0, keepdims=True)
    sol_four = apply_block(top_rhs[4:6] - top_update[4:6] - acc_four, top_inv[4:6])
    acc_top = acc_top + apply_block(sol_four, top_low[8:10]).sum(0, keepdims=True)
    sol_five = apply_block(top_rhs[6:7] - top_update[6:7] - acc_top, top_inv[6:7])
    return jnp.stack(solved, axis=0), jnp.concatenate([sol_three, sol_four, sol_five], axis=0)
```

```python
import functools

import jax
import jax.numpy as jnp
from jax import lax
from jax.experimental import pallas as pl
from jax.experimental.pallas import tpu as pltpu
from jax.sharding import PartitionSpec as P

BLOCK = 128
MESH = pl.DeviceIdType.MESH


def apply_block(vectors, matrices):
    return jnp.einsum("btc,brc->btr", vectors, matrices, precision=lax.Precision.HIGH)


def place():
    return lax.axis_index("leaf"), lax.axis_index("row"), lax.axis_index("col")


def remote(src, dst, send, recv, target):
    return pltpu.make_async_remote_copy(
        src_ref=src, dst_ref=dst, send_sem=send, recv_sem=recv, device_id=target, device_id_type=MESH
    )


def reduce_kernel(cols, x_ref, o_ref, got, pair, send, recv, pair_send, pair_recv):
    leaf, row, col = place()
    per = cols // 2
    width = o_ref.shape[-1]
    holds = col // per == row
    barrier = pltpu.get_barrier_semaphore()

    @pl.when(holds)
    def _():
        for d in range(1, cols):
            pl.semaphore_signal(
                barrier, inc=1, device_id=(leaf, row, lax.rem(col + d, cols)), device_id_type=MESH
            )

    @pl.when(jnp.logical_not(holds))
    def _():
        pl.semaphore_signal(barrier, inc=1, device_id=(leaf, 1 - row, col), device_id_type=MESH)

    pl.semaphore_wait(barrier, per)

    def out_copy(j):
        return remote(
            x_ref.at[:, :, j * width : (j + 1) * width],
            got.at[col],
            send.at[j],
            recv.at[col],
            (leaf, row, row * per + j),
        )

    for j in range(per):
        @pl.when(row * per + j != col)
        def _():
            out_copy(j).start()

    across = remote(o_ref, pair, pair_send, pair_recv, (leaf, 1 - row, col))

    @pl.when(holds)
    def _():
        for j in range(per):
            @pl.when(row * per + j == col)
            def _():
                o_ref[...] = x_ref[:, :, j * width : (j + 1) * width]
        for d in range(1, cols):
            source = lax.rem(col + d, cols)
            remote(
                got.at[source], got.at[source], send.at[0], recv.at[source], (leaf, row, source)
            ).wait_recv()
            o_ref[...] += got[source]
        across.start()
        across.wait_send()

    @pl.when(jnp.logical_not(holds))
    def _():
        across.wait_recv()
        o_ref[...] = pair[...]

    for j in range(per):
        @pl.when(row * per + j != col)
        def _():
            out_copy(j).wait_send()


def gather_kernel(cols, x_ref, o_ref, got, send, recv):
    leaf, row, col = place()
    per = cols // 2
    width = x_ref.shape[-1]
    holds = col // per == row
    barrier = pltpu.get_barrier_semaphore()
    slot = lax.rem(col, per)
    for j in range(per):
        @pl.when(row * per + j != col)
        def _():
            pl.semaphore_signal(
                barrier, inc=1, device_id=(leaf, row, row * per + j), device_id_type=MESH
            )

    def out_copy(d):
        return remote(
            x_ref, got.at[slot], send.at[d - 1], recv.at[slot], (leaf, row, lax.rem(col + d, cols))
        )

    @pl.when(holds)
    def _():
        pl.semaphore_wait(barrier, cols - 1)
        for d in range(1, cols):
            out_copy(d).start()

    for j in range(per):
        part = slice(j * width, (j + 1) * width)

        @pl.when(row * per + j == col)
        def _():
            o_ref[:, :, part] = x_ref[...]

        @pl.when(row * per + j != col)
        def _():
            remote(
                x_ref, got.at[j], send.at[0], recv.at[j], (leaf, row, row * per + j)
            ).wait_recv()
            o_ref[:, :, part] = got[j]

    @pl.when(holds)
    def _():
        for d in range(1, cols):
            out_copy(d).wait_send()


def leaves_kernel(leaves, x_ref, o_ref, got, send, recv):
    leaf, row, col = place()
    barrier = pltpu.get_barrier_semaphore()
    for d in range(1, leaves):
        pl.semaphore_signal(
            barrier, inc=1, device_id=(lax.rem(leaf + d, leaves), row, col), device_id_type=MESH
        )
    pl.semaphore_wait(barrier, leaves - 1)
    copies = []
    for d in range(1, leaves):
        copies.append(
            remote(
                x_ref, got.at[leaf], send.at[d - 1], recv.at[leaf], (lax.rem(leaf + d, leaves), row, col)
            )
        )
        copies[-1].start()
    o_ref[leaf] = x_ref[...]
    for d in range(1, leaves):
        source = lax.rem(leaf + d, leaves)
        remote(x_ref, got.at[source], send.at[0], recv.at[source], (source, row, col)).wait_recv()
        o_ref[source] = got[source]
    for copy in copies:
        copy.wait_send()


def swap_kernel(x_ref, o_ref, got, send, recv):
    leaf, row, col = place()
    barrier = pltpu.get_barrier_semaphore()
    pl.semaphore_signal(barrier, inc=1, device_id=(leaf, 1 - row, col), device_id_type=MESH)
    pl.semaphore_wait(barrier, 1)
    copy = remote(x_ref, got, send, recv, (leaf, 1 - row, col))
    copy.start()
    copy.wait()
    o_ref[...] = got[...]


def call(kernel, x, out_shape, scratch, collective_id):
    return pl.pallas_call(
        kernel,
        out_shape=jax.ShapeDtypeStruct(out_shape, jnp.float32),
        in_specs=[pl.BlockSpec(memory_space=pltpu.VMEM)],
        out_specs=pl.BlockSpec(memory_space=pltpu.VMEM),
        scratch_shapes=scratch,
        compiler_params=pltpu.CompilerParams(
            collective_id=collective_id, has_side_effects=True, vmem_limit_bytes=40 * 1024 * 1024
        ),
    )(x)


DMA = pltpu.SemaphoreType.DMA


def reduce_chunk(x):
    cols = lax.axis_size("col")
    count, nrhs, rows = x.shape
    shape = (count, nrhs, rows // (cols // 2))
    scratch = [
        pltpu.VMEM((cols,) + shape, jnp.float32),
        pltpu.VMEM(shape, jnp.float32),
        DMA((cols // 2,)),
        DMA((cols,)),
        DMA,
        DMA,
    ]
    return call(functools.partial(reduce_kernel, cols), x, shape, scratch, count)


def gather_rows(x, collective_id):
    cols = lax.axis_size("col")
    per = cols // 2
    count, nrhs, width = x.shape
    scratch = [pltpu.VMEM((per,) + x.shape, jnp.float32), DMA((cols - 1,)), DMA((per,))]
    return call(
        functools.partial(gather_kernel, cols), x, (count, nrhs, width * per), scratch, collective_id
    )


def all_leaves(x):
    leaves = lax.axis_size("leaf")
    shape = (leaves,) + x.shape
    scratch = [pltpu.VMEM(shape, jnp.float32), DMA((leaves - 1,)), DMA((leaves,))]
    return call(functools.partial(leaves_kernel, leaves), x, shape, scratch, 10 + x.shape[0])


def swap(x, collective_id):
    return call(swap_kernel, x, x.shape, [pltpu.VMEM(x.shape, jnp.float32), DMA, DMA], collective_id)


def per_device(
    sec_rhs, sec_inv, sec_low, sec_top, sec_rows, top_rhs, top_inv, top_low, sec_parent, top_parent
):
    parts_row = lax.axis_size("row")
    here_leaf, here_row, here_col = place()
    rows_here = sec_rhs.shape[-1]
    cols_here = sec_inv.shape[-1]
    width = rows_here * parts_row
    blocks = width // BLOCK
    nrhs = sec_rhs.shape[2]
    per = rows_here // cols_here
    first = here_col == 0

    def level(known, partial_value, inverse):
        y = reduce_chunk(jnp.where(first, known, 0.0) - partial_value)
        return reduce_chunk(apply_block(y, inverse))

    right_side = sec_rhs[0]
    inverse = sec_inv[0]
    lower = sec_low[0]
    part = lax.dynamic_slice_in_dim(
        right_side[0:4], lax.rem(here_col, per) * cols_here, cols_here, 2
    )
    theirs = swap(
        lax.dynamic_slice_in_dim(right_side[0:4], lax.rem(here_col, per) * cols_here, cols_here, 2), 20
    )
    y_leaf = jnp.where(here_col // per == here_row, part, theirs)
    x_leaf = reduce_chunk(apply_block(y_leaf, inverse[0:4]))
    acc_mid = apply_block(x_leaf, lower[0:4]).reshape(2, 2, nrhs, rows_here).sum(1)
    acc_root = apply_block(x_leaf, lower[4:8]).sum(0, keepdims=True)
    x_mid = level(right_side[4:6], acc_mid, inverse[4:6])
    acc_root = acc_root + apply_block(x_mid, lower[8:10]).sum(0, keepdims=True)
    x_root = level(right_side[6:7], acc_root, inverse[6:7])
    all_cols = jnp.concatenate([x_leaf, x_mid, x_root], axis=0)
    sec_out = gather_rows(all_cols, 21)[None]

    block_rows = sec_top.shape[2] // BLOCK
    contrib = apply_block(all_cols, sec_top[0]).reshape(7, nrhs, block_rows, BLOCK)
    mine = lax.dynamic_slice_in_dim(sec_rows[0], here_row * block_rows, block_rows, 1)
    one_hot = (mine[:, :, None] == jnp.arange(3 * blocks, dtype=jnp.int32)).astype(jnp.float32)
    one_hot = one_hot.reshape(7, block_rows, 3, parts_row, blocks // parts_row)
    spread = jnp.einsum("jtkl,jknpm->pntml", contrib, one_hot, precision=lax.Precision.HIGH)
    spread = spread.reshape(parts_row, 3, nrhs, rows_here)
    path = lax.dynamic_index_in_dim(spread, here_row, 0, keepdims=False) + swap(
        lax.dynamic_index_in_dim(spread, 1 - here_row, 0, keepdims=False), 22
    )

    section_ids = jnp.arange(sec_parent.shape[0], dtype=jnp.int32)
    nodes = jnp.arange(4, dtype=jnp.int32)
    parent_node = jnp.sum(jnp.where(section_ids == here_leaf, sec_parent, 0))
    grands = jnp.sum(jnp.where(sec_parent[:, None] == nodes[None, :], top_parent[None, :], 0), axis=1)
    grand_node = jnp.sum(jnp.where(section_ids == here_leaf, grands, 0))
    owner = jnp.sum(((grands == grand_node) & (section_ids < here_leaf)).astype(jnp.int32)) == 0

    def pick(array, index, count=1):
        return lax.dynamic_slice_in_dim(array, index, count, 0)

    x_three = level(pick(top_rhs, parent_node), path[0:1], pick(top_inv, parent_node))
    reaches = apply_block(
        jnp.broadcast_to(x_three, (2,) + x_three.shape[1:]), pick(top_low, 2 * parent_node, 2)
    )
    mid_known = jnp.where(first & owner, pick(top_rhs, 4 + grand_node), 0.0)
    y_four = all_leaves(reduce_chunk(mid_known - path[1:2] - reaches[0:1]))
    same = (grands == grand_node)[:, None, None, None]
    y_four = jnp.sum(jnp.where(same, y_four, 0.0), axis=0)
    x_four = reduce_chunk(apply_block(y_four, pick(top_inv, 4 + grand_node)))
    acc_top = apply_block(x_four, pick(top_low, 8 + grand_node))
    root_known = jnp.where(first & (here_leaf == 0), top_rhs[6:7], 0.0)
    y_five = all_leaves(
        reduce_chunk(root_known - path[2:3] - reaches[1:2] - jnp.where(owner, acc_top, 0.0))
    ).sum(0)
    x_five = reduce_chunk(apply_block(y_five, top_inv[6:7]))

    both = all_leaves(jnp.concatenate([x_three, x_four], axis=0))
    tops = []
    for p in range(4):
        tops.append(jnp.sum(jnp.where((sec_parent == p)[:, None, None], both[:, 0], 0.0), axis=0))
    for q in range(2):
        at = (grands == q) & (
            jnp.cumsum((grands == q).astype(jnp.int32)) == 1
        )
        tops.append(jnp.sum(jnp.where(at[:, None, None], both[:, 1], 0.0), axis=0))
    top_out = gather_rows(jnp.concatenate([jnp.stack(tops), x_five], axis=0), 21)
    return (sec_out, top_out)


def solution(mesh):
    placed = (
        P("leaf", None, None, "row"),
        P("leaf", None, "row", "col"),
        P("leaf", None, "row", "col"),
        P("leaf", None, "row", "col"),
        P("leaf", None, None),
        P(None, None, "row"),
        P(None, "row", "col"),
        P(None, "row", "col"),
        P(),
        P(),
    )
    return jax.shard_map(
        per_device,
        mesh=mesh,
        in_specs=placed,
        out_specs=(P("leaf", None, None, "row"), P(None, None, "row")),
        check_vma=False,
    )
```
